32 devices in a mesh: dp: 4 (over y, core), expert: 8 (over z, x).
Axes of the slice: x: 2, y: 2, z: 4, core: 2. Of those that a mesh axis runs over, the one named last changes fastest.
Arguments:
- tokens: bfloat16 [4096, 2048], P(('dp', 'expert')), may hold values from -6 to 6
- cotangent: bfloat16 [4096, 2048], P(('dp', 'expert')), may hold values from -6 to 6
- gate_probs: float32 [4096, 8], P(('dp', 'expert')), may hold values from 0.05 to 0.5
- routes: int32 [4096, 8], P(('dp', 'expert')), may hold values from 0 to 15, all different within a row; in each aligned block of 128 rows (0 to 127, 128 to 255, ...) at most 96 rows name the same one
- w_in: bfloat16 [32, 1024, 384], P(('expert', 'dp')), may hold values from -0.125 to 0.125
- w_out: bfloat16 [32, 192, 2048], P(('expert', 'dp')), may hold values from -0.3125 to 0.3125
- mom_in: float32 [32, 1024, 384], P(('expert', 'dp')), may hold values from -48 to 48
- mom_out: float32 [32, 192, 2048], P(('expert', 'dp')), may hold values from -48 to 48
Outputs:
- input_grad: bfloat16 [4096, 2048], P(('dp', 'expert'))
- new_mom_in: float32 [32, 1024, 384], P(('expert', 'dp'))
- new_mom_out: float32 [32, 192, 2048], P(('expert', 'dp'))
The draws below stay inside these ranges and needn't reach their ends.
Inputs may be any that keep to these rules, and one draw needn't show every extreme that they name: `routes`: each row names 8 different experts; within the rows of one device no expert is named more than 96 times, a bound that some block reaches.
All inputs are finite; a program needn't handle non-finite values.
Results may differ from the reference program's by a relative error of at most 0.0064.
Values may be sent and summed in bfloat16 or wider, within the bound.
No kernel may reach another device: no remote copies, remote signals or barrier semaphores. Data moves between devices by JAX's collectives and lax.ppermute only.
A program may use at most 128 MiB of HBM per device.

```python
import math
import jax
import jax.numpy as jnp
import numpy as np
from jax import lax

D = 2048
FF = 384
TOP = 8
TOK_DEV = 128
E = 16
CAP = 96
TOKENS = 4096


def level_of(rng, shape, cuts, least, high):
    def one(position, blocks):
        steps = jax.random.uniform(jax.random.fold_in(jax.random.fold_in(rng, 6), position), (blocks,), jnp.float32, least / len(cuts), high / len(cuts))
        return jnp.repeat(jnp.exp(steps), shape[position] // blocks).reshape((-1,) + (1,) * (len(shape) - position - 1))

    gain = one(*cuts[0])
    for cut in cuts[1:]:
        gain = gain * one(*cut)
    return gain


def deal_out(rng, own, number, rows, amount, top, most, lean):
    ranking = jax.random.permutation(rng, amount)
    heavy_load, common = shares(amount, rows * top, most, lean, True), shares(amount, rows * top, most, lean, False)
    places = jnp.arange(amount)

    def named(sizes, rotation):
        used = int((sizes > 0).sum())
        fixed = max(1, used // 4)
        moved = fixed + (places - fixed + rotation * (used - fixed)) % max(1, amount - fixed)
        return jnp.zeros((amount,), jnp.int32).at[ranking[jnp.where(places < fixed, places, moved)]].set(jnp.asarray(sizes, jnp.int32))

    sizes = jnp.where(number % 4 == 0, named(heavy_load, number // 4), named(common, number - number // 4 - 1))
    mixed = jax.random.permutation(jax.random.fold_in(own, 3), amount)
    giver, receiver = mixed[0:amount // 2 * 2:2], mixed[1:amount // 2 * 2:2]
    margin = jnp.minimum(sizes[giver] - 1, most - sizes[receiver]) // 2
    margin = jnp.where((giver == ranking[0]) | (receiver == ranking[0]) | (sizes[receiver] == 0), 0, jnp.maximum(margin, 0))
    moved = jax.random.randint(jax.random.fold_in(own, 4), (amount // 2,), 0, 1 << 20) % (margin + 1)
    sizes = sizes.at[giver].add(-moved).at[receiver].add(moved)
    items = jnp.searchsorted(jnp.cumsum(sizes), jnp.arange(rows * top), side="right").astype(jnp.int32)
    table = items.reshape(top, rows).T
    table = table[jax.random.permutation(jax.random.fold_in(own, 1), rows)]
    rotation = jax.random.randint(jax.random.fold_in(own, 2), (rows, 1), 0, top)
    return jnp.take_along_axis(table, (jnp.arange(top)[None, :] + rotation) % top, axis=1)


def shares(amount, total, bound, skew, full):
    weights = [(1 << 20) // math.isqrt(grade ** skew) + 1 for grade in range(1, amount + 1)]
    largest = bound if full else min(bound, max(-(-total // amount), total * weights[0] // sum(weights)))
    least = 1 if total - largest >= amount - 1 else 0
    given, spare = [largest] + [least] * (amount - 1), total - largest - least * (amount - 1)
    while spare > 0:
        candidates = [i for i in range(1, amount) if given[i] < largest] or [i for i in range(1, amount) if given[i] < bound]
        mass, budget = sum([weights[i] for i in candidates]), spare
        for i in candidates:
            extra = min(bound - given[i], max(1, budget * weights[i] // mass), spare)
            given[i] = given[i] + extra
            spare = spare - extra
    return np.array(given)


def scatter_about(rng, shape, deviation, bound, pieces=(), held_as=jnp.bfloat16):
    gain = level_of(rng, shape, pieces, -0.22, 0.18) if pieces else 1.0
    result = jax.random.normal(rng, shape, jnp.float32) * deviation * gain
    return jnp.minimum(jnp.maximum(result, -bound), bound).astype(held_as)


def setup_inputs(seed: int = 0) -> dict:
    arg_keys = jax.random.split(jax.random.key(seed), 9)
    tokens = scatter_about(arg_keys[0], (TOKENS, D), 1.0, 6.0, ((0, 32),))
    cotangent = scatter_about(arg_keys[1], (TOKENS, D), 1.0, 6.0, ((0, 32),))
    gate_probs = jnp.clip(jnp.exp(math.log(0.5) - 2.3025851 * jax.random.uniform(arg_keys[2], (TOKENS, TOP), jnp.float32) ** level_of(arg_keys[2], (TOKENS, TOP), ((0, 32),), -0.2, 0.2)), 0.05, 0.5)
    routes_keys = jax.random.split(jax.random.fold_in(arg_keys[3], 1), TOKENS // TOK_DEV)
    routes_turns = jax.random.permutation(jax.random.fold_in(arg_keys[3], 3), TOKENS // TOK_DEV)
    routes = jax.vmap(lambda own, number: deal_out(jax.random.fold_in(arg_keys[3], 2), own, number, TOK_DEV, E, TOP, CAP, 2))(routes_keys, routes_turns).reshape((TOKENS, TOP))
    w_in = scatter_about(arg_keys[4], (2 * E, D // 2, FF), D ** -0.5, 0.125, ((0, 32),))
    w_out = scatter_about(arg_keys[5], (2 * E, FF // 2, D), FF ** -0.5, 0.3125, ((0, 32),))
    mom_in = scatter_about(arg_keys[6], (2 * E, D // 2, FF), 8.0, 48.0, ((0, 32),), jnp.float32)
    mom_out = scatter_about(arg_keys[7], (2 * E, FF // 2, D), 8.0, 48.0, ((0, 32),), jnp.float32)
    return dict(tokens=tokens, cotangent=cotangent, gate_probs=gate_probs, routes=routes, w_in=w_in, w_out=w_out, mom_in=mom_in, mom_out=mom_out)


momentum_beta = 0.9


def slots_of(block_row):
    onehot = (block_row[:, None] == jnp.arange(E, dtype=jnp.int32)[None, :]).astype(jnp.int32)
    return jnp.sum((jnp.cumsum(onehot, axis=0) - 1) * onehot, axis=1).astype(jnp.int32)


def reference(tokens, cotangent, gate_probs, routes, w_in, w_out, mom_in, mom_out):
    blocks = TOKENS // TOK_DEV
    per_block = TOK_DEV * TOP
    flat_route = routes.reshape(blocks, per_block)
    slot_all = lax.map(slots_of, flat_route)
    buffer_len = blocks * CAP
    block_ids = jnp.arange(blocks, dtype=jnp.int32)[:, None]
    where_to = (flat_route * buffer_len + block_ids * CAP + slot_all).astype(jnp.int32)
    assign_ids = jnp.arange(TOKENS * TOP, dtype=jnp.int32)
    lookup = jnp.full((E * buffer_len,), TOKENS * TOP, jnp.int32)
    lookup = lookup.at[where_to.reshape(-1)].set(assign_ids).reshape(E, buffer_len)
    tokens_pad = jnp.concatenate([tokens, jnp.zeros((1, D), tokens.dtype)], 0)
    cot_pad = jnp.concatenate([cotangent, jnp.zeros((1, D), cotangent.dtype)], 0)
    probs_pad = jnp.concatenate([gate_probs.reshape(-1), jnp.zeros((1,), gate_probs.dtype)], 0)
    full_in = w_in.reshape(E, D, FF)
    full_out = w_out.reshape(E, FF, D)
    moment_in = mom_in.reshape(E, D, FF)
    moment_out = mom_out.reshape(E, FF, D)

    def expert_step(accum, inputs):
        slot_ids, weight_in, weight_out, prior_in, prior_out = inputs
        token_idx = (slot_ids // TOP).astype(jnp.int32)
        rows_x = tokens_pad[token_idx]
        scaled = (probs_pad[slot_ids][:, None] * cot_pad[token_idx].astype(jnp.float32)).astype(jnp.bfloat16)
        pre_act = jnp.dot(rows_x, weight_in, preferred_element_type=jnp.float32)
        sigmoid_v = jax.nn.sigmoid(pre_act)
        hidden = (pre_act * sigmoid_v).astype(jnp.bfloat16)
        back_h = lax.dot_general(scaled, weight_out, (((1,), (1,)), ((), ())), preferred_element_type=jnp.float32)
        d_pre = (back_h * sigmoid_v * (1.0 + pre_act * (1.0 - sigmoid_v))).astype(jnp.bfloat16)
        dx_rows = lax.dot_general(d_pre, weight_in, (((1,), (1,)), ((), ())), preferred_element_type=jnp.float32).astype(jnp.bfloat16)
        grad_out = lax.dot_general(hidden, scaled, (((0,), (0,)), ((), ())), preferred_element_type=jnp.float32)
        grad_in = lax.dot_general(rows_x, d_pre, (((0,), (0,)), ((), ())), preferred_element_type=jnp.float32)
        accum = accum.at[token_idx].add(dx_rows.astype(jnp.float32))
        return accum, (momentum_beta * prior_in + grad_in, momentum_beta * prior_out + grad_out)

    start = jnp.zeros((TOKENS + 1, D), jnp.float32)
    accum, (new_in, new_out) = lax.scan(expert_step, start, (lookup, full_in, full_out, moment_in, moment_out))
    input_grad = accum[:TOKENS].astype(jnp.bfloat16)
    return input_grad, new_in.reshape(2 * E, D // 2, FF), new_out.reshape(2 * E, FF // 2, D)
```

```python
import jax
import jax.numpy as jnp
from jax import lax
from jax.sharding import PartitionSpec as P

momentum_beta = 0.9
f32 = jnp.float32
bf16 = jnp.bfloat16


def ring_order(n, nx):
    nz = n // nx
    if n % nx or nx < 2 or nz < 2 or nz % 2:
        return list(range(n))
    order = []
    for z in range(nz):
        xs = list(range(1, nx))
        order += [z * nx + x for x in (xs if z % 2 == 0 else xs[::-1])]
    return order + [z * nx for z in reversed(range(nz))]


def after(x, *others):
    return lax.optimization_barrier((x,) + others)[0]


def per_device(tokens, cotangent, gate_probs, routes, w_in, w_out, mom_in, mom_out):
    n_data = lax.axis_size("dp")
    n = lax.axis_size("expert")
    ny = n_data // 2
    tok, width = tokens.shape
    half = tok // 2
    ff = w_in.shape[2]
    core = lax.axis_index("dp") % 2
    y_idx = lax.axis_index("dp") // 2
    ex = lax.axis_index("expert")
    lower = core == 0

    order = ring_order(n, ny)
    place = [order.index(i) for i in range(n)]

    def ring(x, step):
        return lax.ppermute(x, "expert", [(i, order[(place[i] + step) % n]) for i in range(n)])

    def swap_core(x):
        return lax.ppermute(x, "dp", [(i, i ^ 1) for i in range(n_data)])

    def shift_y(x, r):
        return lax.ppermute(x, "dp", [(i, (i // 2 + r) % ny * 2 + i % 2) for i in range(n_data)])

    top = routes.shape[1]
    parts, rest = [], gate_probs
    for _ in range(3):
        part = lax.reduce_precision(rest, 8, 7)
        parts.append(part)
        rest = rest - part
    lanes = -(-4 * top // 128) * 128
    side = jnp.concatenate(parts + [routes.astype(f32), jnp.zeros((tok, lanes - 4 * top), f32)], 1)
    cot_side = jnp.concatenate([cotangent, side.astype(bf16)], 1)
    column = lax.broadcasted_iota(jnp.int32, (1, ny * ff), 1)

    def gate_of(side):
        side = side.astype(f32)
        gate = side[:, :top] + side[:, top : 2 * top] + side[:, 2 * top : 3 * top]
        named = side[:, 3 * top : 4 * top]
        out = None
        for r in range(ny):
            expert = (ex * ny + (y_idx + r) % ny).astype(f32)
            p = jnp.sum(jnp.where(named == expert, gate, 0.0), axis=1, keepdims=True)
            out = p if out is None else jnp.where(column < r * ff, out, p)
        return jnp.broadcast_to(out, (side.shape[0], ny * ff))

    far = n // 2
    got_x, got_c = {0: tokens}, {0: cot_side}

    def pass_on(got, s):
        if s < far:
            got[-s], got[s] = ring(got[1 - s], 1), ring(got[s - 1], -1)
        else:
            fwd, bwd = ring(got[1 - s][:half], 1), ring(got[s - 1][half:], -1)
            got[s] = jnp.concatenate([fwd, bwd], 0)

    full_in = jnp.zeros((width, ny * ff), bf16)
    wout_rows = []
    rows_in = w_in.shape[1]

    def weights(r, full_in, tie):
        a, b = w_in[0], w_out[0]
        if r:
            a, b = shift_y(a, -r), shift_y(b, -r)
        oa, ob = swap_core(after(a, *tie)), swap_core(after(b, *tie))
        for piece, at in ((a, core), (oa, 1 - core)):
            full_in = lax.dynamic_update_slice(full_in, piece, (at * rows_in, r * ff))
        wout_rows.append(jnp.concatenate([jnp.where(lower, b, ob), jnp.where(lower, ob, b)], 0))
        return full_in

    span = max(1, n // 8)
    groups = [[0]]
    for s in range(1, far, span):
        groups.append([d for t in range(s, min(s + span, far)) for d in (-t, t)])
    groups.append([far])

    def within(step):
        return sum(max(group) <= step for group in groups)

    xs, cs, hs, ds, dxs = [], [], [], [], {}

    def work(group, full_in, full_out):
        x = jnp.concatenate([got_x[d] for d in group], 0)
        c = jnp.concatenate([got_c[d][:, :width] for d in group], 0)
        prob = gate_of(jnp.concatenate([got_c[d][:, width:] for d in group], 0))
        pre = jnp.dot(x, full_in, preferred_element_type=f32)
        back = lax.dot_general(c, full_out, (((1,), (1,)), ((), ())), preferred_element_type=f32)
        sig = jax.nn.sigmoid(pre)
        hid = (prob * pre * sig).astype(bf16)
        d_pre = (prob * back * sig * (1.0 + pre * (1.0 - sig))).astype(bf16)
        dx = lax.dot_general(d_pre, full_in, (((1,), (1,)), ((), ())), preferred_element_type=f32)
        for i, d in enumerate(group):
            dxs[d] = dx[i * tok : (i + 1) * tok].astype(f32 if n <= 16 else bf16)
        xs.append(x)
        cs.append(c)
        hs.append(hid)
        ds.append(d_pre)

    tn = (((0,), (0,)), ((), ()))
    grads = {}

    def add_up(which, r, block, *others):
        cols = slice(r * ff, (r + 1) * ff)
        p, q = (hs, cs) if which == "out" else (xs, ds)
        p, q = jnp.concatenate(p[block], 0), jnp.concatenate(q[block], 0)
        if which == "out":
            p = after(p[:, cols], *others)
        else:
            q = after(q[:, cols], *others)
        g = lax.dot_general(p, q, tn, preferred_element_type=f32)
        grads[which, r] = g + grads[which, r] if (which, r) in grads else g

    pairs = [(which, r) for r in list(range(1, ny)) + [0] for which in ("out", "in")]
    done = 0

    def work_up_to(count):
        nonlocal done
        while done < count:
            tie = tuple(grads.values()) if span > 1 else ()
            work(groups[done], after(full_in, *tie), full_out)
            done += 1
            if span > 1 and done < len(groups):
                for which, r in pairs:
                    add_up(which, r, slice(done - 1, done))
        return [dxs[d] for d in groups[done - 1]]

    def hold(got, s, *others):
        for d in (s, -s) if 0 < s < far else (s,):
            got[d] = after(got[d], *others)

    for s in range(1, far + 1):
        if s == min(3, far):
            for r in range(ny):
                tie = (got_c[min(2, s - 1)], got_c[-min(2, s - 1)]) if r else (got_x[1], got_x[-1])
                full_in = weights(r, full_in, tie)
            full_out = jnp.concatenate(wout_rows, 0)
        if s == far and far > 2:
            hold(got_x, far - 1, *work_up_to(within(far - 3)))
        pass_on(got_x, s)
        if s == far and far > 2:
            hold(got_c, far - 1, *work_up_to(within(far - 2)))
        pass_on(got_c, s)

    cut = within(far - 2)
    if span == 1 and cut:
        for which, r in pairs:
            add_up(which, r, slice(0, cut))
    hold(got_c, far, *grads.values())
    work_up_to(len(groups))
    last = dxs[far].astype(bf16)
    sums = {}
    for which, r in pairs:
        add_up(which, r, slice(cut if span == 1 else len(groups) - 1, None), last)
        g = grads[which, r]
        rows = g.shape[0] // 2
        keep = lax.dynamic_slice_in_dim(g, core * rows, rows, 0)
        give = lax.dynamic_slice_in_dim(g, (1 - core) * rows, rows, 0).astype(bf16)
        part = keep + swap_core(give).astype(f32)
        sums[which, r] = part.astype(bf16) if r else part
    early = [sums[which, r] for which in ("out", "in") for r in range(1, ny)]
    theirs = {(which, r): shift_y(sums[which, r], r) for which, r in pairs if r}

    def flow(lo, hi, sign, start):
        acc = dxs[sign * start if start < far else far][lo:hi].astype(bf16)
        for d in range(start - 1, -1, -1):
            acc = ring(acc, sign)
            if d == far - 1:
                acc = after(acc, *early)
            if d == min(far - 2, 1):
                acc = after(acc, *[theirs["out", r] for r in range(1, ny)])
            acc = acc.astype(f32)
            if d:
                acc = (acc + dxs[sign * d][lo:hi]).astype(bf16)
        return acc

    upper = flow(0, half, 1, far) + flow(0, half, -1, far - 1) + dxs[0][:half]
    under = flow(half, tok, -1, far) + flow(half, tok, 1, far - 1) + dxs[0][half:]
    input_grad = jnp.concatenate([upper, under], 0).astype(bf16)

    new = {}
    for which, mom in (("out", mom_out), ("in", mom_in)):
        total = sums[which, 0]
        for r in range(1, ny):
            total = total + theirs[which, r].astype(f32)
        new[which] = (momentum_beta * mom[0] + total)[None]
    return (input_grad, new["in"], new["out"])


def solution(mesh):
    rows = P(("dp", "expert"), None)
    entries = P(("expert", "dp"), None, None)
    return jax.shard_map(
        per_device,
        mesh=mesh,
        in_specs=(rows,) * 4 + (entries,) * 4,
        out_specs=(rows, entries, entries),
        check_vma=False,
    )
```

```python
import jax
import jax.numpy as jnp
from jax import lax
from jax.experimental import pallas as pl
from jax.experimental.pallas import tpu as pltpu
from jax.sharding import PartitionSpec as P

momentum_beta = 0.9
f32 = jnp.float32
bf16 = jnp.bfloat16


def ring_order(n, nx):
    nz = n // nx
    if n % nx or nx < 2 or nz < 2 or nz % 2:
        return list(range(n))
    order = []
    for z in range(nz):
        xs = list(range(1, nx))
        order += [z * nx + x for x in (xs if z % 2 == 0 else xs[::-1])]
    return order + [z * nx for z in reversed(range(nz))]


def after(x, *others):
    return lax.optimization_barrier((x,) + others)[0]


def pack(tokens, cotangent, gate_probs, routes, experts):
    tok, width = tokens.shape
    top = routes.shape[1]
    half = tok // 2
    lanes = -(-3 * experts // 128) * 128

    def kernel(tok_ref, cot_ref, gate_ref, route_ref, *outs):
        gate = gate_ref[...].T
        route = route_ref[...].astype(f32).T
        lane = lax.broadcasted_iota(jnp.int32, (tok, lanes), 1)
        part = sum((lane >= i * experts).astype(jnp.int32) for i in range(1, 4))
        expert = (lane - part * experts).astype(f32)
        p = jnp.zeros((tok, lanes), f32)
        for j in range(top):
            p = jnp.where(route[:, j : j + 1] == expert, gate[:, j : j + 1], p)
        high = p.astype(bf16).astype(f32)
        middle = (p - high).astype(bf16).astype(f32)
        low = p - high - middle
        side = jnp.where(part == 0, high, jnp.where(part == 1, middle, jnp.where(part == 2, low, 0.0)))
        for i, out in enumerate(outs):
            rows = slice(i * half, (i + 1) * half)
            out[:, :width] = tok_ref[rows, :]
            out[:, width : 2 * width] = cot_ref[rows, :]
            out[:, 2 * width :] = side[rows, :].astype(bf16)

    return pl.pallas_call(
        kernel,
        out_shape=[jax.ShapeDtypeStruct((half, 2 * width + lanes), bf16)] * 2,
        cost_estimate=pl.CostEstimate(flops=0, bytes_accessed=8 * tok * width, transcendentals=0),
    )(tokens, cotangent, gate_probs.T, routes.T)


NT = (((1,), (1,)), ((), ()))
TN = (((0,), (0,)), ((), ()))
hint = pl.CostEstimate(flops=1 << 20, bytes_accessed=1 << 16, transcendentals=0)


def expert_rows(rows, ids, full_in, full_out, ny, experts):
    width, n_ff = full_in.shape
    ff = n_ff // ny
    total = sum(part.shape[0] for part in rows)
    lanes = rows[0].shape[1] - 2 * width

    def kernel(id_ref, in_ref, out_ref, *refs):
        row_refs, (hid_ref, pre_ref, dx_ref, x_ref, c_ref, gate_ref) = refs[: len(rows)], refs[len(rows) :]
        at = 0
        for ref in row_refs:
            here = slice(at, at + ref.shape[0])
            at += ref.shape[0]
            x_ref[here, :] = ref[:, :width]
            c_ref[here, :] = ref[:, width : 2 * width]
            side = ref[:, 2 * width :].astype(f32)
            lane = lax.broadcasted_iota(jnp.int32, side.shape, 1)
            for r in range(ny):
                own = id_ref[r]
                named = (lane == own) | (lane == own + experts) | (lane == own + 2 * experts)
                p = jnp.sum(jnp.where(named, side, 0.0), axis=1, keepdims=True)
                gate_ref[here, r * 128 : (r + 1) * 128] = jnp.broadcast_to(p, (side.shape[0], 128))
        for t in range(0, n_ff, 256):
            cols = slice(t, min(t + 256, n_ff))
            pre = jnp.dot(x_ref[...], in_ref[:, cols], preferred_element_type=f32)
            back = lax.dot_general(c_ref[...], out_ref[cols, :], NT, preferred_element_type=f32)
            gates = [gate_ref[:, u // ff * 128 : u // ff * 128 + 128] for u in range(cols.start, cols.stop, 128)]
            gate = jnp.concatenate(gates, 1)
            sig = jax.nn.sigmoid(pre)
            hid_ref[:, cols] = (gate * pre * sig).astype(bf16)
            pre_ref[:, cols] = (gate * back * sig * (1.0 + pre * (1.0 - sig))).astype(bf16)
        for t in range(0, width, 512):
            cols = slice(t, min(t + 512, width))
            dx = lax.dot_general(pre_ref[...], in_ref[cols, :], NT, preferred_element_type=f32)
            dx_ref[:, cols] = dx.astype(bf16)

    need = 2 * (4 * width * n_ff + total * (6 * width + lanes + 2 * n_ff)) + 4 * total * (2 * width + ny * 128)
    return pl.pallas_call(
        kernel,
        in_specs=[pl.BlockSpec(memory_space=pltpu.SMEM)] + [pl.BlockSpec(memory_space=pltpu.VMEM)] * (2 + len(rows)),
        out_shape=[
            jax.ShapeDtypeStruct((total, n_ff), bf16),
            jax.ShapeDtypeStruct((total, n_ff), bf16),
            jax.ShapeDtypeStruct((total, width), bf16),
            jax.ShapeDtypeStruct((total, width), bf16),
            jax.ShapeDtypeStruct((total, width), bf16),
        ],
        scratch_shapes=[pltpu.VMEM((total, ny * 128), f32)],
        compiler_params=pltpu.CompilerParams(vmem_limit_bytes=min(need + (8 << 20), 58 << 20)),
        cost_estimate=hint,
    )(ids, full_in, full_out, *rows)


def per_device(tokens, cotangent, gate_probs, routes, w_in, w_out, mom_in, mom_out):
    n_data = lax.axis_size("dp")
    n = lax.axis_size("expert")
    ny = n_data // 2
    tok, width = tokens.shape
    half = tok // 2
    ff = w_in.shape[2]
    core = lax.axis_index("dp") % 2
    y_idx = lax.axis_index("dp") // 2
    ex = lax.axis_index("expert")
    lower = core == 0

    order = ring_order(n, ny)
    place = [order.index(i) for i in range(n)]

    def ring(x, step):
        return lax.ppermute(x, "expert", [(i, order[(place[i] + step) % n]) for i in range(n)])

    def swap_core(x):
        return lax.ppermute(x, "dp", [(i, i ^ 1) for i in range(n_data)])

    def shift_y(x, r):
        return lax.ppermute(x, "dp", [(i, (i // 2 + r) % ny * 2 + i % 2) for i in range(n_data)])

    experts = n * ny
    mine = pack(tokens, cotangent, gate_probs, routes, experts)
    ids = ex * ny + (y_idx + jnp.arange(ny, dtype=jnp.int32)) % ny

    far = n // 2
    got = {0: list(mine)}

    def pass_on(s):
        if s < far:
            got[-s] = [ring(part, 1) for part in got[1 - s]]
            got[s] = [ring(part, -1) for part in got[s - 1]]
        else:
            got[s] = [ring(got[1 - s][0], 1), ring(got[s - 1][1], -1)]

    def both(s):
        return got[-s] + got[s]

    def hold(s, *others):
        for d in (s, -s) if s < far else (s,):
            got[d] = [after(part, *others) for part in got[d]]

    def gather_in():
        full = jnp.zeros((width, ny * ff), bf16)
        rows = w_in.shape[1]
        for r in range(ny):
            own = shift_y(after(w_in[0], mine[0]), -r) if r else w_in[0]
            if r and far > 1:
                hold(1, own)
            other = swap_core(after(own, *both(1)) if far > 1 else own)
            for piece, at in ((own, core), (other, 1 - core)):
                full = lax.dynamic_update_slice(full, piece, (at * rows, r * ff))
        return full

    def gather_out():
        full = []
        for r in range(ny):
            own = w_out[0]
            if r:
                own = shift_y(after(own, *both(1)) if far > 1 else own, -r)
            own = after(own, *both(2)) if far > 2 else own
            other = swap_core(own)
            full += [jnp.where(lower, own, other), jnp.where(lower, other, own)]
        return jnp.concatenate(full, 0)

    if n <= 16:
        groups = [[0] + [d for t in range(1, far - 1) for d in (-t, t)], [d for d in (1 - far, far - 1) if d] + [far]]
    else:
        groups = [[0]]
        for s in range(1, far, n // 8):
            groups.append([d for t in range(s, min(s + n // 8, far)) for d in (-t, t)])
        groups.append([far])

    def within(step):
        return sum(max(group) <= step for group in groups)

    held, dxs = [], {}

    def work(group, full_in, full_out):
        tie = []
        if max(group) < far - 1 and far > 2:
            tie = both(far - 2) if n <= 16 else both(max(group) + 1)
        rows = [after(part, *tie) for d in group for part in got[d]]
        hid, d_pre, dx, x, c = expert_rows(rows, ids, full_in, full_out, ny, experts)
        for i, d in enumerate(group):
            dxs[d] = dx[i * tok : (i + 1) * tok]
        held.append((x, c, hid, d_pre))

    grads = {}

    def add_up(r, arrays, *others):
        x, c, hid, d_pre = arrays
        cols = slice(r * ff, (r + 1) * ff)
        for which, p, q in (("out", hid[:, cols], c), ("in", x, d_pre[:, cols])):
            g = lax.dot_general(after(p, *others), q, TN, preferred_element_type=f32)
            grads[which, r] = g + grads[which, r] if (which, r) in grads else g

    def to_core(r):
        for which in ("out", "in"):
            g = grads[which, r]
            rows = g.shape[0] // 2
            keep = lax.dynamic_slice_in_dim(g, core * rows, rows, 0)
            give = lax.dynamic_slice_in_dim(g, (1 - core) * rows, rows, 0).astype(bf16)
            sums[which, r] = keep + swap_core(give).astype(f32)

    sums = {}
    at_once = range(1, ny) if n <= 16 else range(ny)
    done = 0

    def work_up_to(count):
        nonlocal done
        while done < count:
            work(groups[done], after(full_in, *grads.values()), full_out)
            done += 1
            if done < len(groups):
                for r in at_once:
                    add_up(r, held[-1])
        return list(grads.values()) + list(dxs.values())

    for s in range(1, far + 1):
        if s == min(2, far):
            full_in = gather_in()
        if s == min(3, far):
            if far > 2:
                hold(2, full_in)
            full_out = gather_out()
        if s == far > 2 and n <= 16:
            hold(s - 1, *work_up_to(within(far - 2)))
        pass_on(s)

    hold(far, *work_up_to(len(groups) - 1))
    work_up_to(len(groups))
    for r in range(1, ny):
        add_up(r, held[-1])
        to_core(r)
        for which in ("out", "in"):
            sums[which, r] = sums[which, r].astype(bf16)

    count = max(1, min(3, far - 1))
    theirs = {key: [] for key in sums if key[1]}

    def piece(key, i):
        unit = -(-sums[key].shape[0] // (16 * count)) * 16
        return sums[key][i * unit : (i + 1) * unit]

    upper, under, ends = slice(0, half), slice(half, tok), []
    flows = [(1, upper, far), (-1, under, far)] + ([(1, under, far - 1), (-1, upper, far - 1)] if far > 1 else [])
    accs = [dxs[sign * d if d < far else d][rows].astype(bf16) for sign, rows, d in flows]
    for step in range(far):
        i = step - 1 if far > 1 else 0
        keys = list(theirs) if 0 <= i < count else []
        sent = [ring(acc, sign) for (sign, _, _), acc in zip(flows, accs)]
        moved = [shift_y(piece(key, i), key[1]) for key in keys]
        tied = [sums[key] for key in theirs] if step == 0 else []
        out = lax.optimization_barrier((sent, moved, tied))
        sent, moved = out[0], out[1]
        if step == 0:
            sums.update(zip(theirs, out[2]))
            for arrays in held if n <= 16 else held[-1:]:
                add_up(0, arrays, *sent)
            to_core(0)
        for key, part in zip(keys, moved):
            theirs[key].append(part)
        following, accs = [], []
        for (sign, rows, d), acc in zip(flows, sent):
            if d > 1:
                following.append((sign, rows, d - 1))
                accs.append((acc.astype(f32) + dxs[sign * (d - 1)][rows]).astype(bf16))
            else:
                ends.append((rows, acc))
        flows = following
    grad = {rows.start: dxs[0][rows].astype(f32) for rows in (upper, under)}
    for rows, acc in ends:
        grad[rows.start] = grad[rows.start] + acc.astype(f32)
    input_grad = jnp.concatenate([grad[0], grad[half]], 0).astype(bf16)

    new = {}
    for which, mom in (("out", mom_out), ("in", mom_in)):
        total = sums[which, 0]
        for r in range(1, ny):
            total = total + jnp.concatenate(theirs[which, r], 0).astype(f32)
        new[which] = (momentum_beta * mom[0] + total)[None]
    return (input_grad, new["in"], new["out"])


def solution(mesh):
    rows = P(("dp", "expert"), None)
    entries = P(("expert", "dp"), None, None)
    return jax.shard_map(
        per_device,
        mesh=mesh,
        in_specs=(rows,) * 4 + (entries,) * 4,
        out_specs=(rows, entries, entries),
        check_vma=False,
    )
```

```python
import jax
import jax.numpy as jnp
from jax import lax
from jax.experimental import pallas as pl
from jax.experimental.pallas import tpu as pltpu
from jax.sharding import PartitionSpec as P

momentum_beta = 0.9
f32 = jnp.float32
bf16 = jnp.bfloat16


def ring_order(n, nx):
    nz = n // nx
    if n % nx or nx < 2 or nz < 2 or nz % 2:
        return list(range(n))
    order = []
    for z in range(nz):
        xs = list(range(1, nx))
        order += [z * nx + x for x in (xs if z % 2 == 0 else xs[::-1])]
    return order + [z * nx for z in reversed(range(nz))]


def after(x, *others):
    return lax.optimization_barrier((x,) + others)[0]


def pack(tokens, cotangent, gate_probs, routes, experts):
    tok, width = tokens.shape
    top = routes.shape[1]
    half = tok // 2
    lanes = -(-3 * experts // 128) * 128

    def kernel(tok_ref, cot_ref, gate_ref, route_ref, *outs):
        gate = gate_ref[...].T
        route = route_ref[...].astype(f32).T
        lane = lax.broadcasted_iota(jnp.int32, (tok, lanes), 1)
        part = sum((lane >= i * experts).astype(jnp.int32) for i in range(1, 4))
        expert = (lane - part * experts).astype(f32)
        p = jnp.zeros((tok, lanes), f32)
        for j in range(top):
            p = jnp.where(route[:, j : j + 1] == expert, gate[:, j : j + 1], p)
        high = p.astype(bf16).astype(f32)
        middle = (p - high).astype(bf16).astype(f32)
        low = p - high - middle
        side = jnp.where(part == 0, high, jnp.where(part == 1, middle, jnp.where(part == 2, low, 0.0)))
        for i, out in enumerate(outs):
            rows = slice(i * half, (i + 1) * half)
            out[:, :width] = tok_ref[rows, :]
            out[:, width : 2 * width] = cot_ref[rows, :]
            out[:, 2 * width :] = side[rows, :].astype(bf16)

    return pl.pallas_call(
        kernel,
        out_shape=[jax.ShapeDtypeStruct((half, 2 * width + lanes), bf16)] * 2,
        cost_estimate=pl.CostEstimate(flops=0, bytes_accessed=8 * tok * width, transcendentals=0),
    )(tokens, cotangent, gate_probs.T, routes.T)


NT = (((1,), (1,)), ((), ()))
TN = (((0,), (0,)), ((), ()))
hint = pl.CostEstimate(flops=1 << 20, bytes_accessed=1 << 16, transcendentals=0)


def expert_rows(rows, ids, full_in, full_out, ny, experts):
    width, n_ff = full_in.shape
    ff = n_ff // ny
    total = sum(part.shape[0] for part in rows)
    lanes = rows[0].shape[1] - 2 * width

    def kernel(id_ref, in_ref, out_ref, *refs):
        row_refs, (hid_ref, pre_ref, dx_ref, x_ref, c_ref, gate_ref) = refs[: len(rows)], refs[len(rows) :]
        at = 0
        for ref in row_refs:
            here = slice(at, at + ref.shape[0])
            at += ref.shape[0]
            x_ref[here, :] = ref[:, :width]
            c_ref[here, :] = ref[:, width : 2 * width]
            side = ref[:, 2 * width :].astype(f32)
            lane = lax.broadcasted_iota(jnp.int32, side.shape, 1)
            for r in range(ny):
                own = id_ref[r]
                named = (lane == own) | (lane == own + experts) | (lane == own + 2 * experts)
                p = jnp.sum(jnp.where(named, side, 0.0), axis=1, keepdims=True)
                gate_ref[here, r * 128 : (r + 1) * 128] = jnp.broadcast_to(p, (side.shape[0], 128))
        for t in range(0, n_ff, 256):
            cols = slice(t, min(t + 256, n_ff))
            pre = jnp.dot(x_ref[...], in_ref[:, cols], preferred_element_type=f32)
            back = lax.dot_general(c_ref[...], out_ref[cols, :], NT, preferred_element_type=f32)
            gates = [gate_ref[:, u // ff * 128 : u // ff * 128 + 128] for u in range(cols.start, cols.stop, 128)]
            gate = jnp.concatenate(gates, 1)
            sig = jax.nn.sigmoid(pre)
            hid_ref[:, cols] = (gate * pre * sig).astype(bf16)
            pre_ref[:, cols] = (gate * back * sig * (1.0 + pre * (1.0 - sig))).astype(bf16)
        for t in range(0, width, 512):
            cols = slice(t, min(t + 512, width))
            dx = lax.dot_general(pre_ref[...], in_ref[cols, :], NT, preferred_element_type=f32)
            dx_ref[:, cols] = dx.astype(bf16)

    need = 2 * (4 * width * n_ff + total * (6 * width + lanes + 2 * n_ff)) + 4 * total * (2 * width + ny * 128)
    return pl.pallas_call(
        kernel,
        in_specs=[pl.BlockSpec(memory_space=pltpu.SMEM)] + [pl.BlockSpec(memory_space=pltpu.VMEM)] * (2 + len(rows)),
        out_shape=[
            jax.ShapeDtypeStruct((total, n_ff), bf16),
            jax.ShapeDtypeStruct((total, n_ff), bf16),
            jax.ShapeDtypeStruct((total, width), bf16),
            jax.ShapeDtypeStruct((total, width), bf16),
            jax.ShapeDtypeStruct((total, width), bf16),
        ],
        scratch_shapes=[pltpu.VMEM((total, ny * 128), f32)],
        compiler_params=pltpu.CompilerParams(vmem_limit_bytes=min(need + (8 << 20), 58 << 20)),
        cost_estimate=hint,
    )(ids, full_in, full_out, *rows)


def per_device(tokens, cotangent, gate_probs, routes, w_in, w_out, mom_in, mom_out):
    n_data = lax.axis_size("dp")
    n = lax.axis_size("expert")
    ny = n_data // 2
    tok, width = tokens.shape
    half = tok // 2
    ff = w_in.shape[2]
    core = lax.axis_index("dp") % 2
    y_idx = lax.axis_index("dp") // 2
    ex = lax.axis_index("expert")
    lower = core == 0

    order = ring_order(n, ny)
    place = [order.index(i) for i in range(n)]

    def ring(x, step):
        return lax.ppermute(x, "expert", [(i, order[(place[i] + step) % n]) for i in range(n)])

    def swap_core(x):
        return lax.ppermute(x, "dp", [(i, i ^ 1) for i in range(n_data)])

    def shift_y(x, r):
        return lax.ppermute(x, "dp", [(i, (i // 2 + r) % ny * 2 + i % 2) for i in range(n_data)])

    experts = n * ny
    mine = pack(tokens, cotangent, gate_probs, routes, experts)
    ids = ex * ny + (y_idx + jnp.arange(ny, dtype=jnp.int32)) % ny

    far = n // 2
    got = {0: list(mine)}

    def pass_on(s):
        if s < far:
            (fwd, fwd_late), (bwd_late, bwd) = got[1 - s], got[s - 1]
            fwd_late, bwd_late = ring(fwd_late, 1), ring(bwd_late, -1)
            got[-s], got[s] = [ring(fwd, 1), fwd_late], [bwd_late, ring(bwd, -1)]
        else:
            got[s] = [ring(got[1 - s][0], 1), ring(got[s - 1][1], -1)]

    def both(s):
        return got[-s] + got[s]

    def hold(s, *others):
        for d in (s, -s) if s < far else (s,):
            got[d] = [after(part, *others) for part in got[d]]

    def gather_in():
        full = jnp.zeros((width, ny * ff), bf16)
        rows = w_in.shape[1]
        for r in range(ny):
            own = shift_y(after(w_in[0], mine[0]), -r) if r else w_in[0]
            if r and far > 1:
                hold(1, own)
            other = swap_core(after(own, *both(1)) if far > 1 else own)
            for piece, at in ((own, core), (other, 1 - core)):
                full = lax.dynamic_update_slice(full, piece, (at * rows, r * ff))
        return full

    def gather_out():
        full = []
        for r in range(ny):
            own = w_out[0]
            if r:
                own = shift_y(after(own, *both(1)) if far > 1 else own, -r)
            own = after(own, *both(2)) if far > 2 else own
            other = swap_core(own)
            full += [jnp.where(lower, own, other), jnp.where(lower, other, own)]
        return jnp.concatenate(full, 0)

    if n <= 16:
        groups = [[0] + [d for t in range(1, far - 1) for d in (-t, t)], [far]]
        if far > 1:
            groups.insert(1, [1 - far, far - 1])
    else:
        groups = [[0]]
        for s in range(1, far, n // 8):
            groups.append([d for t in range(s, min(s + n // 8, far)) for d in (-t, t)])
        groups.append([far])

    def within(step):
        return sum(max(group) <= step for group in groups)

    held, dxs = [], {}

    def work(group, full_in, full_out):
        tie = []
        if max(group) < far - 1 and far > 2:
            tie = both(far - 2) if n <= 16 else both(max(group) + 1)
        halves = sorted(((d, i) for d in group for i in range(2)), key=lambda at: at[0] * (2 * at[1] - 1) > 0)
        rows = [after(got[d][i], *tie) for d, i in halves]
        hid, d_pre, dx, x, c = expert_rows(rows, ids, full_in, full_out, ny, experts)
        for at, (d, i) in enumerate(halves):
            dxs[d, i] = dx[at * half : (at + 1) * half]
        held.append((x, c, hid, d_pre))

    grads = {}

    def add_up(r, arrays, *others):
        x, c, hid, d_pre = lax.optimization_barrier((arrays, others))[0] if others else arrays
        cols = slice(r * ff, (r + 1) * ff)
        for which, p, q in (("out", hid[:, cols], c), ("in", x, d_pre[:, cols])):
            g = lax.dot_general(p, q, TN, preferred_element_type=f32)
            grads[which, r] = g + grads[which, r] if (which, r) in grads else g

    def to_core(r):
        for which in ("out", "in"):
            g = grads[which, r]
            rows = g.shape[0] // 2
            keep = lax.dynamic_slice_in_dim(g, core * rows, rows, 0)
            give = lax.dynamic_slice_in_dim(g, (1 - core) * rows, rows, 0).astype(bf16)
            sums[which, r] = keep + swap_core(give).astype(f32)

    sums = {}
    at_once = range(1, ny) if n <= 16 else range(ny)
    done = 0

    def work_up_to(count):
        nonlocal done
        while done < count:
            work(groups[done], after(full_in, *grads.values()), full_out)
            done += 1
            if done < len(groups):
                for r in at_once:
                    add_up(r, held[-1])
        return list(dxs.values())

    for s in range(1, far + 1):
        if s == min(2, far):
            full_in = gather_in()
        if s == min(3, far):
            if far > 2:
                hold(2, full_in)
            full_out = gather_out()
        if s == far > 2 and n <= 16:
            hold(s - 1, *work_up_to(within(far - 2)))
        pass_on(s)

    hold(far, *work_up_to(len(groups) - 1), *grads.values())
    work_up_to(len(groups))
    for r in range(1, ny):
        add_up(r, held[-1])
        to_core(r)
        for which in ("out", "in"):
            sums[which, r] = sums[which, r].astype(bf16)

    count = max(1, min(3, far - 1))
    theirs = {key: [] for key in sums if key[1]}

    def piece(key, i):
        unit = -(-sums[key].shape[0] // (16 * count)) * 16
        return sums[key][i * unit : (i + 1) * unit]

    ends = []
    flows = [(1, 0, far), (-1, 1, far)] + ([(1, 1, far - 1), (-1, 0, far - 1)] if far > 1 else [])
    accs = [dxs[sign * d if d < far else d, i] for sign, i, d in flows]
    for step in range(far):
        i = step - 1 if far > 1 else 0
        keys = list(theirs) if 0 <= i < count else []
        sent = [ring(acc, sign) for (sign, _, _), acc in zip(flows, accs)]
        moved = [shift_y(piece(key, i), key[1]) for key in keys]
        tied = [sums[key] for key in theirs] if step == 0 else []
        out = lax.optimization_barrier((sent, moved, tied))
        sent, moved = out[0], out[1]
        if step == 0:
            sums.update(zip(theirs, out[2]))
            for arrays in held if n <= 16 else held[-1:]:
                add_up(0, arrays, *sent)
            to_core(0)
        for key, part in zip(keys, moved):
            theirs[key].append(part)
        following, accs = [], []
        for (sign, part, d), acc in zip(flows, sent):
            if d > 1:
                following.append((sign, part, d - 1))
                accs.append((acc.astype(f32) + dxs[sign * (d - 1), part]).astype(bf16))
            else:
                ends.append((part, acc))
        flows = following
    grad = [dxs[0, 0].astype(f32), dxs[0, 1].astype(f32)]
    for part, acc in ends:
        grad[part] = grad[part] + acc.astype(f32)
    input_grad = jnp.concatenate(grad, 0).astype(bf16)

    new = {}
    for which, mom in (("out", mom_out), ("in", mom_in)):
        total = sums[which, 0]
        for r in range(1, ny):
            total = total + jnp.concatenate(theirs[which, r], 0).astype(f32)
        new[which] = (momentum_beta * mom[0] + total)[None]
    return (input_grad, new["in"], new["out"])


def solution(mesh):
    rows = P(("dp", "expert"), None)
    entries = P(("expert", "dp"), None, None)
    return jax.shard_map(
        per_device,
        mesh=mesh,
        in_specs=(rows,) * 4 + (entries,) * 4,
        out_specs=(rows, entries, entries),
        check_vma=False,
    )
```

```python
import jax
import jax.numpy as jnp
from jax import lax
from jax.experimental import pallas as pl
from jax.experimental.pallas import tpu as pltpu
from jax.sharding import PartitionSpec as P

momentum_beta = 0.9
f32 = jnp.float32
bf16 = jnp.bfloat16


def ring_order(n, nx):
    nz = n // nx
    if n % nx or nx < 2 or nz < 2 or nz % 2:
        return list(range(n))
    order = []
    for z in range(nz):
        xs = list(range(1, nx))
        order += [z * nx + x for x in (xs if z % 2 == 0 else xs[::-1])]
    return order + [z * nx for z in reversed(range(nz))]


def after(x, *others):
    return lax.optimization_barrier((x,) + others)[0]


def pack(tokens, cotangent, gate_probs, routes, experts):
    tok, width = tokens.shape
    top = routes.shape[1]
    half = tok // 2
    lanes = -(-3 * experts // 128) * 128

    def kernel(tok_ref, cot_ref, gate_ref, route_ref, *outs):
        gate = gate_ref[...].T
        route = route_ref[...].astype(f32).T
        lane = lax.broadcasted_iota(jnp.int32, (tok, lanes), 1)
        part = sum((lane >= i * experts).astype(jnp.int32) for i in range(1, 4))
        expert = (lane - part * experts).astype(f32)
        p = jnp.zeros((tok, lanes), f32)
        for j in range(top):
            p = jnp.where(route[:, j : j + 1] == expert, gate[:, j : j + 1], p)
        high = p.astype(bf16).astype(f32)
        middle = (p - high).astype(bf16).astype(f32)
        low = p - high - middle
        side = jnp.where(part == 0, high, jnp.where(part == 1, middle, jnp.where(part == 2, low, 0.0)))
        for i, out in enumerate(outs):
            rows = slice(i * half, (i + 1) * half)
            out[:, :width] = tok_ref[rows, :]
            out[:, width : 2 * width] = cot_ref[rows, :]
            out[:, 2 * width :] = side[rows, :].astype(bf16)

    return pl.pallas_call(
        kernel,
        out_shape=[jax.ShapeDtypeStruct((half, 2 * width + lanes), bf16)] * 2,
        cost_estimate=pl.CostEstimate(flops=0, bytes_accessed=8 * tok * width, transcendentals=0),
    )(tokens, cotangent, gate_probs.T, routes.T)


NT = (((1,), (1,)), ((), ()))
TN = (((0,), (0,)), ((), ()))
hint = pl.CostEstimate(flops=1 << 20, bytes_accessed=1 << 16, transcendentals=0)


def expert_rows(rows, ids, full_in, full_out, ny, experts):
    width, n_ff = full_in.shape
    ff = n_ff // ny
    total = sum(part.shape[0] for part in rows)
    lanes = rows[0].shape[1] - 2 * width

    def kernel(id_ref, in_ref, out_ref, *refs):
        row_refs, (hid_ref, pre_ref, dx_ref, x_ref, c_ref, gate_ref) = refs[: len(rows)], refs[len(rows) :]
        at = 0
        for ref in row_refs:
            here = slice(at, at + ref.shape[0])
            at += ref.shape[0]
            x_ref[here, :] = ref[:, :width]
            c_ref[here, :] = ref[:, width : 2 * width]
            side = ref[:, 2 * width :].astype(f32)
            lane = lax.broadcasted_iota(jnp.int32, side.shape, 1)
            for r in range(ny):
                own = id_ref[r]
                named = (lane == own) | (lane == own + experts) | (lane == own + 2 * experts)
                p = jnp.sum(jnp.where(named, side, 0.0), axis=1, keepdims=True)
                gate_ref[here, r * 128 : (r + 1) * 128] = jnp.broadcast_to(p, (side.shape[0], 128))
        for t in range(0, n_ff, 256):
            cols = slice(t, min(t + 256, n_ff))
            pre = jnp.dot(x_ref[...], in_ref[:, cols], preferred_element_type=f32)
            back = lax.dot_general(c_ref[...], out_ref[cols, :], NT, preferred_element_type=f32)
            gates = [gate_ref[:, u // ff * 128 : u // ff * 128 + 128] for u in range(cols.start, cols.stop, 128)]
            gate = jnp.concatenate(gates, 1)
            sig = jax.nn.sigmoid(pre)
            hid_ref[:, cols] = (gate * pre * sig).astype(bf16)
            pre_ref[:, cols] = (gate * back * sig * (1.0 + pre * (1.0 - sig))).astype(bf16)
        for t in range(0, width, 512):
            cols = slice(t, min(t + 512, width))
            dx = lax.dot_general(pre_ref[...], in_ref[cols, :], NT, preferred_element_type=f32)
            dx_ref[:, cols] = dx.astype(bf16)

    need = 2 * (4 * width * n_ff + total * (6 * width + lanes + 2 * n_ff)) + 4 * total * (2 * width + ny * 128)
    return pl.pallas_call(
        kernel,
        in_specs=[pl.BlockSpec(memory_space=pltpu.SMEM)] + [pl.BlockSpec(memory_space=pltpu.VMEM)] * (2 + len(rows)),
        out_shape=[
            jax.ShapeDtypeStruct((total, n_ff), bf16),
            jax.ShapeDtypeStruct((total, n_ff), bf16),
            jax.ShapeDtypeStruct((total, width), bf16),
            jax.ShapeDtypeStruct((total, width), bf16),
            jax.ShapeDtypeStruct((total, width), bf16),
        ],
        scratch_shapes=[pltpu.VMEM((total, ny * 128), f32)],
        compiler_params=pltpu.CompilerParams(vmem_limit_bytes=min(need + (8 << 20), 58 << 20)),
        cost_estimate=hint,
    )(ids, full_in, full_out, *rows)


def per_device(tokens, cotangent, gate_probs, routes, w_in, w_out, mom_in, mom_out):
    n_data = lax.axis_size("dp")
    n = lax.axis_size("expert")
    ny = n_data // 2
    tok, width = tokens.shape
    half = tok // 2
    ff = w_in.shape[2]
    core = lax.axis_index("dp") % 2
    y_idx = lax.axis_index("dp") // 2
    ex = lax.axis_index("expert")
    lower = core == 0

    order = ring_order(n, ny)
    place = [order.index(i) for i in range(n)]

    def ring(x, step):
        return lax.ppermute(x, "expert", [(i, order[(place[i] + step) % n]) for i in range(n)])

    def swap_core(x):
        return lax.ppermute(x, "dp", [(i, i ^ 1) for i in range(n_data)])

    def shift_y(x, r):
        return lax.ppermute(x, "dp", [(i, (i // 2 + r) % ny * 2 + i % 2) for i in range(n_data)])

    experts = n * ny
    mine = pack(tokens, cotangent, gate_probs, routes, experts)
    ids = ex * ny + (y_idx + jnp.arange(ny, dtype=jnp.int32)) % ny

    far = n // 2
    got = {0: list(mine)}

    def pass_on(s):
        if s < far:
            (fwd, fwd_late), (bwd_late, bwd) = got[1 - s], got[s - 1]
            fwd_late, bwd_late = ring(fwd_late, 1), ring(bwd_late, -1)
            got[-s], got[s] = [ring(fwd, 1), fwd_late], [bwd_late, ring(bwd, -1)]
        else:
            got[s] = [ring(got[1 - s][0], 1), ring(got[s - 1][1], -1)]

    def both(s):
        return got[-s] + got[s]

    def hold(s, *others):
        for d in (s, -s) if s < far else (s,):
            got[d] = [after(part, *others) for part in got[d]]

    def gather_in():
        full = jnp.zeros((width, ny * ff), bf16)
        rows = w_in.shape[1]
        for r in range(ny):
            own = shift_y(after(w_in[0], mine[0]), -r) if r else w_in[0]
            if r and far > 1:
                hold(1, own)
            other = swap_core(after(own, *both(1)) if far > 1 else own)
            for piece, at in ((own, core), (other, 1 - core)):
                full = lax.dynamic_update_slice(full, piece, (at * rows, r * ff))
        return full

    def gather_out():
        full = []
        for r in range(ny):
            own = w_out[0]
            if r:
                own = shift_y(after(own, *both(1)) if far > 1 else own, -r)
            own = after(own, *both(2)) if far > 2 else own
            other = swap_core(own)
            full += [jnp.where(lower, own, other), jnp.where(lower, other, own)]
        return jnp.concatenate(full, 0)

    if n <= 16:
        groups = [[0] + [d for t in range(1, far - 1) for d in (-t, t)], [far]]
        if far > 1:
            groups.insert(1, [1 - far, far - 1])
    else:
        groups = [[0]]
        for s in range(1, far, n // 8):
            groups.append([d for t in range(s, min(s + n // 8, far)) for d in (-t, t)])
        groups.append([far])

    def within(step):
        return sum(max(group) <= step for group in groups)

    held, dxs = [], {}

    def work(group, full_in, full_out):
        tie = []
        if max(group) < far - 1 and far > 2:
            tie = both(far - 2) if n <= 16 else both(max(group) + 1)
        halves = sorted(((d, i) for d in group for i in range(2)), key=lambda at: at[0] * (2 * at[1] - 1) > 0)
        rows = [after(got[d][i], *tie) for d, i in halves]
        hid, d_pre, dx, x, c = expert_rows(rows, ids, full_in, full_out, ny, experts)
        for at, (d, i) in enumerate(halves):
            dxs[d, i] = dx[at * half : (at + 1) * half]
        held.append((x, c, hid, d_pre))

    grads = {}

    def add_up(r, arrays, *others):
        x, c, hid, d_pre = lax.optimization_barrier((arrays, others))[0] if others else arrays
        cols = slice(r * ff, (r + 1) * ff)
        for which, p, q in (("out", hid[:, cols], c), ("in", x, d_pre[:, cols])):
            g = lax.dot_general(p, q, TN, preferred_element_type=f32)
            grads[which, r] = g + grads[which, r] if (which, r) in grads else g

    def to_core(r):
        for which in ("out", "in"):
            g = grads[which, r]
            rows = g.shape[0] // 2
            keep = lax.dynamic_slice_in_dim(g, core * rows, rows, 0)
            give = lax.dynamic_slice_in_dim(g, (1 - core) * rows, rows, 0).astype(bf16)
            sums[which, r] = keep + swap_core(give).astype(f32)

    sums = {}
    at_once = range(1, ny) if n <= 16 else range(ny)
    done = 0

    def work_up_to(count):
        nonlocal done
        while done < count:
            work(groups[done], after(full_in, *grads.values()) if n > 16 else full_in, full_out)
            done += 1
            if done < len(groups):
                for r in at_once:
                    add_up(r, held[-1])
        return list(dxs.values())

    for s in range(1, far + 1):
        if s == min(2, far):
            full_in = gather_in()
        if s == min(3, far):
            if far > 2:
                got[-2][1], got[2][0] = after(got[-2][1], full_in), after(got[2][0], full_in)
            full_out = gather_out()
        if s == far > 2 and n <= 16:
            hold(s - 1, *work_up_to(within(far - 2)))
        pass_on(s)

    hold(far, *work_up_to(len(groups) - 1), *grads.values())
    work_up_to(len(groups))
    for r in range(1, ny):
        add_up(r, held[-1])
        to_core(r)
        for which in ("out", "in"):
            sums[which, r] = sums[which, r].astype(bf16)

    count = max(1, min(3, far - 1))
    theirs = {key: [] for key in sums if key[1]}

    def piece(key, i):
        unit = -(-sums[key].shape[0] // (16 * count)) * 16
        return sums[key][i * unit : (i + 1) * unit]

    ends = []
    flows = [(1, 0, far), (-1, 1, far)] + ([(1, 1, far - 1), (-1, 0, far - 1)] if far > 1 else [])
    accs = [dxs[sign * d if d < far else d, i] for sign, i, d in flows]
    for step in range(far):
        i = step - 1 if far > 1 else 0
        keys = list(theirs) if 0 <= i < count else []
        sent = [ring(acc, sign) for (sign, _, _), acc in zip(flows, accs)]
        moved = [shift_y(piece(key, i), key[1]) for key in keys]
        tied = [sums[key] for key in theirs] if step == 0 else []
        out = lax.optimization_barrier((sent, moved, tied))
        sent, moved = out[0], out[1]
        if step == 0:
            sums.update(zip(theirs, out[2]))
            for arrays in held if n <= 16 else held[-1:]:
                add_up(0, arrays, *sent)
            to_core(0)
        for key, part in zip(keys, moved):
            theirs[key].append(part)
        following, accs = [], []
        for (sign, part, d), acc in zip(flows, sent):
            if d > 1:
                following.append((sign, part, d - 1))
                accs.append((acc.astype(f32) + dxs[sign * (d - 1), part]).astype(bf16))
            else:
                ends.append((part, acc))
        flows = following
    grad = [dxs[0, 0].astype(f32), dxs[0, 1].astype(f32)]
    for part, acc in ends:
        grad[part] = grad[part] + acc.astype(f32)
    input_grad = jnp.concatenate(grad, 0).astype(bf16)

    new = {}
    for which, mom in (("out", mom_out), ("in", mom_in)):
        total = sums[which, 0]
        for r in range(1, ny):
            total = total + jnp.concatenate(theirs[which, r], 0).astype(f32)
        new[which] = (momentum_beta * mom[0] + total)[None]
    return (input_grad, new["in"], new["out"])


def solution(mesh):
    rows = P(("dp", "expert"), None)
    entries = P(("expert", "dp"), None, None)
    return jax.shard_map(
        per_device,
        mesh=mesh,
        in_specs=(rows,) * 4 + (entries,) * 4,
        out_specs=(rows, entries, entries),
        check_vma=False,
    )
```

```python
import jax
import jax.numpy as jnp
from jax import lax
from jax.experimental import pallas as pl
from jax.experimental.pallas import tpu as pltpu
from jax.sharding import PartitionSpec as P

momentum_beta = 0.9
f32 = jnp.float32
bf16 = jnp.bfloat16


def ring_order(n, nx):
    nz = n // nx
    if n % nx or nx < 2 or nz < 2 or nz % 2:
        return list(range(n))
    order = []
    for z in range(nz):
        xs = list(range(1, nx))
        order += [z * nx + x for x in (xs if z % 2 == 0 else xs[::-1])]
    return order + [z * nx for z in reversed(range(nz))]


def after(x, *others):
    return lax.optimization_barrier((x,) + others)[0]


def pack(tokens, cotangent, gate_probs, routes, experts):
    tok, width = tokens.shape
    top = routes.shape[1]
    half = tok // 2
    lanes = -(-3 * experts // 128) * 128

    def kernel(tok_ref, cot_ref, gate_ref, route_ref, *outs):
        gate = gate_ref[...].T
        route = route_ref[...].astype(f32).T
        lane = lax.broadcasted_iota(jnp.int32, (tok, lanes), 1)
        part = sum((lane >= i * experts).astype(jnp.int32) for i in range(1, 4))
        expert = (lane - part * experts).astype(f32)
        p = jnp.zeros((tok, lanes), f32)
        for j in range(top):
            p = jnp.where(route[:, j : j + 1] == expert, gate[:, j : j + 1], p)
        high = p.astype(bf16).astype(f32)
        middle = (p - high).astype(bf16).astype(f32)
        low = p - high - middle
        side = jnp.where(part == 0, high, jnp.where(part == 1, middle, jnp.where(part == 2, low, 0.0)))
        for i, out in enumerate(outs):
            rows = slice(i * half, (i + 1) * half)
            out[:, :width] = tok_ref[rows, :]
            out[:, width : 2 * width] = cot_ref[rows, :]
            out[:, 2 * width :] = side[rows, :].astype(bf16)

    return pl.pallas_call(
        kernel,
        out_shape=[jax.ShapeDtypeStruct((half, 2 * width + lanes), bf16)] * 2,
        cost_estimate=pl.CostEstimate(flops=0, bytes_accessed=8 * tok * width, transcendentals=0),
    )(tokens, cotangent, gate_probs.T, routes.T)


NT = (((1,), (1,)), ((), ()))
TN = (((0,), (0,)), ((), ()))
hint = pl.CostEstimate(flops=1 << 20, bytes_accessed=1 << 16, transcendentals=0)


def expert_rows(rows, ids, full_in, full_out, ny, experts):
    width, n_ff = full_in.shape
    ff = n_ff // ny
    total = sum(part.shape[0] for part in rows)
    lanes = rows[0].shape[1] - 2 * width

    def kernel(id_ref, in_ref, out_ref, *refs):
        row_refs, (hid_ref, pre_ref, dx_ref, x_ref, c_ref, gate_ref) = refs[: len(rows)], refs[len(rows) :]
        at = 0
        for ref in row_refs:
            here = slice(at, at + ref.shape[0])
            at += ref.shape[0]
            x_ref[here, :] = ref[:, :width]
            c_ref[here, :] = ref[:, width : 2 * width]
            side = ref[:, 2 * width :].astype(f32)
            lane = lax.broadcasted_iota(jnp.int32, side.shape, 1)
            for r in range(ny):
                own = id_ref[r]
                named = (lane == own) | (lane == own + experts) | (lane == own + 2 * experts)
                p = jnp.sum(jnp.where(named, side, 0.0), axis=1, keepdims=True)
                gate_ref[here, r * 128 : (r + 1) * 128] = jnp.broadcast_to(p, (side.shape[0], 128))
        for t in range(0, n_ff, 256):
            cols = slice(t, min(t + 256, n_ff))
            pre = jnp.dot(x_ref[...], in_ref[:, cols], preferred_element_type=f32)
            back = lax.dot_general(c_ref[...], out_ref[cols, :], NT, preferred_element_type=f32)
            gates = [gate_ref[:, u // ff * 128 : u // ff * 128 + 128] for u in range(cols.start, cols.stop, 128)]
            gate = jnp.concatenate(gates, 1)
            sig = jax.nn.sigmoid(pre)
            hid_ref[:, cols] = (gate * pre * sig).astype(bf16)
            pre_ref[:, cols] = (gate * back * sig * (1.0 + pre * (1.0 - sig))).astype(bf16)
        for t in range(0, width, 512):
            cols = slice(t, min(t + 512, width))
            dx = lax.dot_general(pre_ref[...], in_ref[cols, :], NT, preferred_element_type=f32)
            dx_ref[:, cols] = dx.astype(bf16)

    need = 2 * (4 * width * n_ff + total * (6 * width + lanes + 2 * n_ff)) + 4 * total * (2 * width + ny * 128)
    return pl.pallas_call(
        kernel,
        in_specs=[pl.BlockSpec(memory_space=pltpu.SMEM)] + [pl.BlockSpec(memory_space=pltpu.VMEM)] * (2 + len(rows)),
        out_shape=[
            jax.ShapeDtypeStruct((total, n_ff), bf16),
            jax.ShapeDtypeStruct((total, n_ff), bf16),
            jax.ShapeDtypeStruct((total, width), bf16),
            jax.ShapeDtypeStruct((total, width), bf16),
            jax.ShapeDtypeStruct((total, width), bf16),
        ],
        scratch_shapes=[pltpu.VMEM((total, ny * 128), f32)],
        compiler_params=pltpu.CompilerParams(vmem_limit_bytes=min(need + (8 << 20), 58 << 20)),
        cost_estimate=hint,
    )(ids, full_in, full_out, *rows)


def per_device(tokens, cotangent, gate_probs, routes, w_in, w_out, mom_in, mom_out):
    n_data = lax.axis_size("dp")
    n = lax.axis_size("expert")
    ny = n_data // 2
    tok, width = tokens.shape
    half = tok // 2
    ff = w_in.shape[2]
    core = lax.axis_index("dp") % 2
    y_idx = lax.axis_index("dp") // 2
    ex = lax.axis_index("expert")
    lower = core == 0

    order = ring_order(n, ny)
    place = [order.index(i) for i in range(n)]

    def ring(x, step):
        return lax.ppermute(x, "expert", [(i, order[(place[i] + step) % n]) for i in range(n)])

    def swap_core(x):
        return lax.ppermute(x, "dp", [(i, i ^ 1) for i in range(n_data)])

    def shift_y(x, r):
        return lax.ppermute(x, "dp", [(i, (i // 2 + r) % ny * 2 + i % 2) for i in range(n_data)])

    experts = n * ny
    mine = pack(tokens, cotangent, gate_probs, routes, experts)
    ids = ex * ny + (y_idx + jnp.arange(ny, dtype=jnp.int32)) % ny

    far = n // 2
    got = {0: list(mine)}

    def pass_on(s):
        if s < far:
            (fwd, fwd_late), (bwd_late, bwd) = got[1 - s], got[s - 1]
            fwd_late, bwd_late = ring(fwd_late, 1), ring(bwd_late, -1)
            got[-s], got[s] = [ring(fwd, 1), fwd_late], [bwd_late, ring(bwd, -1)]
        else:
            got[s] = [ring(got[1 - s][0], 1), ring(got[s - 1][1], -1)]

    def both(s):
        return got[-s] + got[s]

    def hold(s, *others):
        for d in (s, -s) if s < far else (s,):
            got[d] = [after(part, *others) for part in got[d]]

    def gather_in():
        full = jnp.zeros((width, ny * ff), bf16)
        rows = w_in.shape[1]
        for r in range(ny):
            own = shift_y(after(w_in[0], mine[0]), -r) if r else w_in[0]
            if r and far > 1:
                hold(1, own)
            other = swap_core(after(own, *both(1)) if far > 1 else own)
            for piece, at in ((own, core), (other, 1 - core)):
                full = lax.dynamic_update_slice(full, piece, (at * rows, r * ff))
        return full

    def gather_out():
        full = []
        for r in range(ny):
            own = w_out[0]
            if r:
                own = shift_y(after(own, *both(1)) if far > 1 else own, -r)
            own = after(own, *both(2)) if far > 2 else own
            other = swap_core(own)
            full += [jnp.where(lower, own, other), jnp.where(lower, other, own)]
        return jnp.concatenate(full, 0)

    if n <= 16:
        groups = [[0] + [d for t in range(1, far - 1) for d in (-t, t)], [far]]
        if far > 1:
            groups.insert(1, [1 - far, far - 1])
    else:
        groups = [[0]]
        for s in range(1, far, n // 8):
            groups.append([d for t in range(s, min(s + n // 8, far)) for d in (-t, t)])
        groups.append([far])

    def within(step):
        return sum(max(group) <= step for group in groups)

    held, dxs = [], {}

    def work(group, full_in, full_out):
        tie = []
        if max(group) < far - 1 and far > 2:
            tie = both(far - 2) if n <= 16 else both(max(group) + 1)
        halves = sorted(((d, i) for d in group for i in range(2)), key=lambda at: at[0] * (2 * at[1] - 1) > 0)
        rows = [after(got[d][i], *tie) for d, i in halves]
        hid, d_pre, dx, x, c = expert_rows(rows, ids, full_in, full_out, ny, experts)
        for at, (d, i) in enumerate(halves):
            dxs[d, i] = dx[at * half : (at + 1) * half]
        held.append((x, c, hid, d_pre))

    grads = {}

    def add_up(r, arrays, *others):
        x, c, hid, d_pre = lax.optimization_barrier((arrays, others))[0] if others else arrays
        cols = slice(r * ff, (r + 1) * ff)
        for which, p, q in (("out", hid[:, cols], c), ("in", x, d_pre[:, cols])):
            g = lax.dot_general(p, q, TN, preferred_element_type=f32)
            grads[which, r] = g + grads[which, r] if (which, r) in grads else g

    def to_core(r):
        for which in ("out", "in"):
            g = grads[which, r]
            rows = g.shape[0] // 2
            keep = lax.dynamic_slice_in_dim(g, core * rows, rows, 0)
            give = lax.dynamic_slice_in_dim(g, (1 - core) * rows, rows, 0).astype(bf16)
            sums[which, r] = keep + swap_core(give).astype(f32)

    sums = {}
    at_once = range(1, ny) if n <= 16 else range(ny)
    done = 0

    def work_up_to(count):
        nonlocal done
        while done < count:
            work(groups[done], after(full_in, *grads.values()) if n > 16 else full_in, full_out)
            done += 1
            if done < len(groups):
                for r in at_once:
                    add_up(r, held[-1])
        return list(dxs.values())

    for s in range(1, far + 1):
        if s == min(2, far):
            full_in = gather_in()
        if s == min(3, far):
            if far > 2:
                got[-2][1], got[2][0] = after(got[-2][1], full_in), after(got[2][0], full_in)
            full_out = gather_out()
        if s == far > 2 and n <= 16:
            hold(s - 1, *work_up_to(within(far - 2)))
        pass_on(s)

    hold(far, *work_up_to(len(groups) - 1), *grads.values())
    work_up_to(len(groups))
    for r in range(1, ny):
        add_up(r, held[-1])
        to_core(r)
        for which in ("out", "in"):
            sums[which, r] = sums[which, r].astype(bf16)

    count = min(4, far)
    theirs = {key: [] for key in sums if key[1]}

    def piece(key, i):
        units = sums[key].shape[0] // 16
        bounds = [0] + [units * (4 * j - 3) // (4 * count - 4) for j in range(1, count)] + [units]
        return sums[key][16 * bounds[i] : 16 * bounds[i + 1]]

    ends = []
    flows = [(1, 0, far), (-1, 1, far)] + ([(1, 1, far - 1), (-1, 0, far - 1)] if far > 1 else [])
    accs = [dxs[sign * d if d < far else d, i] for sign, i, d in flows]
    for step in range(far):
        keys = list(theirs) if step < count else []
        sent = [ring(acc, sign) for (sign, _, _), acc in zip(flows, accs)]
        moved = [shift_y(piece(key, step), key[1]) for key in keys]
        tied = [sums[key] for key in theirs] if step == 0 else []
        out = lax.optimization_barrier((sent, moved, tied))
        sent, moved = out[0], out[1]
        if step == 0:
            sums.update(zip(theirs, out[2]))
            for arrays in held if n <= 16 else held[-1:]:
                add_up(0, arrays, *sent)
            to_core(0)
        for key, part in zip(keys, moved):
            theirs[key].append(part)
        following, accs = [], []
        for (sign, part, d), acc in zip(flows, sent):
            if d > 1:
                following.append((sign, part, d - 1))
                accs.append((acc.astype(f32) + dxs[sign * (d - 1), part]).astype(bf16))
            else:
                ends.append((part, acc))
        flows = following
    grad = [dxs[0, 0].astype(f32), dxs[0, 1].astype(f32)]
    for part, acc in ends:
        grad[part] = grad[part] + acc.astype(f32)
    input_grad = jnp.concatenate(grad, 0).astype(bf16)

    new = {}
    for which, mom in (("out", mom_out), ("in", mom_in)):
        total = sums[which, 0]
        for r in range(1, ny):
            total = total + jnp.concatenate(theirs[which, r], 0).astype(f32)
        new[which] = (momentum_beta * mom[0] + total)[None]
    return (input_grad, new["in"], new["out"])


def solution(mesh):
    rows = P(("dp", "expert"), None)
    entries = P(("expert", "dp"), None, None)
    return jax.shard_map(
        per_device,
        mesh=mesh,
        in_specs=(rows,) * 4 + (entries,) * 4,
        out_specs=(rows, entries, entries),
        check_vma=False,
    )
```
